1024 devices in a mesh: node: 32 (over z), local: 8 (over x, core), cuts: 4 (over y).
Axes of the slice: x: 4, y: 4, z: 32, core: 2. Of those that a mesh axis runs over, the one named last changes fastest.
Arguments:
- tokens: bfloat16 [4096, 2048], P('node'), may hold values from -6 to 6
- expert_ids: int32 [4096, 8], P('node'), may hold values from 0 to 127, as said below
- route_weight: float32 [4096, 8], P('node'), may hold values from 0.25 to 1
- gate_weight: bfloat16 [128, 2048, 1536], P(('node', 'cuts'), None, 'local'), may hold values from -0.125 to 0.125
- up_weight: bfloat16 [128, 2048, 1536], P(('node', 'cuts'), None, 'local'), may hold values from -0.125 to 0.125
- down_weight: bfloat16 [128, 1536, 2048], P(('node', 'cuts'), 'local'), may hold values from -0.15625 to 0.15625
Outputs:
- mixed: bfloat16 [4096, 2048], P('node', ('local', 'cuts'))
The draws below stay inside these ranges and needn't reach their ends.
Inputs may be any that keep to these rules, and one draw needn't show every extreme that they name: `expert_ids`: each token names 8 different experts, lying in at most 4 groups (expert e belongs to group e // 4). In each aligned block of 128 tokens no expert and no group is named by more than 16 tokens, and some expert by exactly 16.
All inputs are finite; a program needn't handle non-finite values.
Results may differ from the reference program's by a relative error of at most 0.02.
Values may be sent and summed in bfloat16 or wider, within the bound.
No kernel may reach another device: no remote copies, remote signals or barrier semaphores. Data moves between devices by JAX's collectives and lax.ppermute only.
A program may use at most 32 MiB of HBM per device.

```python
import math
import jax
import jax.numpy as jnp
from jax import lax

D = 2048
FF = 1536
TOP = 8
TOK_NODE = 128
NODES = 32
EXP_NODE = 4
EXPERTS = 128
FF_DEV = 192
CAP = 16
TOKENS = 4096


def shuffle_nodes(subkey):
    return jax.random.permutation(subkey, NODES)


def draw_expert_ids(key, part):
    key = jax.random.fold_in(key, 11)
    subkeys = jax.random.split(key, 5)
    round_rows = NODES // 4
    round_count = TOKENS // round_rows
    perm_keys = jax.random.split(subkeys[0], round_count)
    orders = jax.vmap(shuffle_nodes)(perm_keys)
    groups = orders.reshape(TOKENS, 4)
    offsets = jnp.arange(EXP_NODE, dtype=jnp.int32)
    candidates = (groups[:, :, None] * EXP_NODE + offsets[None, None, :]).reshape(TOKENS, 4 * EXP_NODE)
    popularity = jax.random.randint(subkeys[1], (EXPERTS,), 0, 48)
    jitter = jax.random.randint(subkeys[2], (TOKENS, 4 * EXP_NODE), 0, 32)
    favorite = jax.random.randint(subkeys[3], (), 0, EXPERTS)
    block_favorite = jax.random.randint(subkeys[4], (TOKENS // TOK_NODE,), 0, EXPERTS)
    row_favorite = jnp.repeat(block_favorite, TOK_NODE)
    favored = (candidates == favorite) | (candidates == row_favorite[:, None])
    scores = jnp.take(popularity, candidates) + jitter + 1000 * favored.astype(jnp.int32)
    scores = scores * 64 + jnp.arange(4 * EXP_NODE, dtype=jnp.int32)[None, :]
    picked = lax.top_k(scores, TOP)[1]
    return jnp.take_along_axis(candidates, picked, axis=1).astype(jnp.int32)


def block_levels(key, shape, cuts, least, largest):
    def one(dim, shards_of):
        heights = jax.random.uniform(jax.random.fold_in(jax.random.fold_in(key, 6), dim), (shards_of,), jnp.float32, least / len(cuts), largest / len(cuts))
        return jnp.repeat(jnp.exp(heights), shape[dim] // shards_of).reshape((-1,) + (1,) * (len(shape) - dim - 1))

    level = one(*cuts[0])
    for cut in cuts[1:]:
        level = level * one(*cut)
    return level


def noise(key, shape, deviation, bound, cuts=(), held_as=jnp.bfloat16):
    entries = jax.random.normal(key, shape, jnp.float32) * deviation
    if len(cuts) > 0:
        entries = block_levels(key, shape, cuts, -0.22, 0.18) * entries
    return jnp.clip(entries, min=-bound, max=bound).astype(held_as)


def setup_inputs(seed: int = 0) -> dict:
    key_list = jax.random.split(jax.random.key(seed), 7)
    return {
        "tokens": noise(key_list[0], (TOKENS, D), 1.0, 6.0, ((0, 32),)),
        "expert_ids": draw_expert_ids(jax.random.fold_in(key_list[6], 71), 0),
        "route_weight": jnp.clip(jnp.exp(math.log(1.0) - 1.3862944 * jax.random.uniform(key_list[2], (TOKENS, TOP), jnp.float32) ** block_levels(key_list[2], (TOKENS, TOP), ((0, 32),), -0.2, 0.2)), 0.25, 1.0),
        "gate_weight": noise(key_list[3], (EXPERTS, D, FF), D ** -0.5, 0.125, ((0, 128), (2, 8))),
        "up_weight": noise(key_list[4], (EXPERTS, D, FF), D ** -0.5, 0.125, ((0, 128), (2, 8))),
        "down_weight": noise(key_list[5], (EXPERTS, FF, D), FF ** -0.5, 0.15625, ((0, 128), (1, 8))),
    }


def reference(tokens, expert_ids, route_weight, gate_weight, up_weight, down_weight):
    capacity_rows = NODES * CAP

    def one_expert(running, expert):
        matches = expert_ids == expert
        chosen = jnp.any(matches, axis=1)
        weights = jnp.sum(jnp.where(matches, route_weight, jnp.float32(0.0)), axis=1)
        row_index = jnp.nonzero(chosen, size=capacity_rows, fill_value=0)[0]
        filled = jnp.arange(capacity_rows) < jnp.sum(chosen.astype(jnp.int32))
        picked = jnp.take(tokens, row_index, axis=0).astype(jnp.float32)
        gate_value = jnp.dot(picked, gate_weight[expert].astype(jnp.float32), preferred_element_type=jnp.float32)
        up_value = jnp.dot(picked, up_weight[expert].astype(jnp.float32), preferred_element_type=jnp.float32)
        hidden = (jax.nn.silu(gate_value) * up_value).astype(jnp.bfloat16)
        hidden_parts = hidden.astype(jnp.float32).reshape(capacity_rows, FF // FF_DEV, FF_DEV)
        down_parts = down_weight[expert].astype(jnp.float32).reshape(FF // FF_DEV, FF_DEV, D)
        partial_value = jnp.einsum("rsf,sfd->srd", hidden_parts, down_parts)
        rounded = lax.optimization_barrier(partial_value.astype(jnp.bfloat16)).astype(jnp.float32)
        summed = jnp.sum(rounded, axis=0)
        factor = jnp.where(filled, jnp.take(weights, row_index), jnp.float32(0.0))
        return running.at[row_index].add(factor[:, None] * summed), None

    start = jnp.zeros((TOKENS, D), jnp.float32)
    mixed, unused = lax.scan(one_expert, start, jnp.arange(EXPERTS, dtype=jnp.int32))
    return mixed.astype(jnp.bfloat16)
```

```python
import functools

import jax
import jax.numpy as jnp
from jax import lax
from jax.experimental import pallas as pl
from jax.experimental.pallas import tpu as pltpu
from jax.sharding import Mesh, PartitionSpec as P

F32 = jnp.float32
BF16 = jnp.bfloat16
NODES = 32
CHIPS = 16
HALF = 8
LANES = 128
WIDTH = 2048
FF = 192
ROWS = NODES * HALF

VMEM = pl.BlockSpec(memory_space=pltpu.VMEM)
SMEM = pl.BlockSpec(memory_space=pltpu.SMEM)
PARAMS = pltpu.CompilerParams(vmem_limit_bytes=40 * 1024 * 1024)


def seat_kernel(where_ref, ids_ref, route_ref, tok_ref, out_ref, pos_ref):
    core = where_ref[0]
    column = where_ref[1]
    tokens = tok_ref.shape[0]
    groups = lax.broadcasted_iota(jnp.int32, (NODES, tokens), 0)
    named = jnp.zeros((NODES, tokens), F32)
    weight = jnp.zeros((NODES, tokens), F32)
    for k in range(ids_ref.shape[0]):
        ids = ids_ref[k : k + 1, :]
        hit = (ids >> 2) == groups
        named = jnp.where(hit, 1.0, named)
        weight = weight + jnp.where(hit & ((ids & 3) == column), route_ref[k : k + 1, :], 0.0)
    before = lax.broadcasted_iota(jnp.int32, (tokens, tokens), 0) < lax.broadcasted_iota(
        jnp.int32, (tokens, tokens), 1
    )
    rank = jnp.dot(named.astype(BF16), before.astype(F32).astype(BF16), preferred_element_type=F32)
    pos = jnp.where(named > 0.0, rank, -1.0)
    pos_ref[...] = pos
    slot = lax.broadcasted_iota(jnp.int32, (1, HALF, 1), 1) + core * HALF
    seated = pos[:, None, :] == slot.astype(F32)
    rows = jnp.where(seated, 1.0, 0.0).reshape(ROWS, tokens).astype(BF16)
    picked = jnp.dot(rows, tok_ref[...], preferred_element_type=F32)
    scale = jnp.sum(jnp.where(seated, weight[:, None, :], 0.0), axis=2, keepdims=True)
    high = scale.astype(BF16).astype(F32)
    lane = lax.broadcasted_iota(jnp.int32, (1, 1, LANES), 2)
    scale = jnp.where(lane < 64, high, scale - high)
    out_ref[:, 0:HALF, :] = picked.reshape(NODES, HALF, LANES).astype(BF16)
    out_ref[:, HALF : 2 * HALF, :] = scale.astype(BF16)


def expert_kernel(x_ref, scale_ref, own_ref, other_ref, out_ref):
    x = jnp.concatenate([x_ref[q] for q in range(CHIPS)], axis=1)
    scale = scale_ref[:, HALF : 2 * HALF, :].reshape(ROWS, LANES).astype(F32)
    scale = scale[:, 0:1] + scale[:, 64:65]
    hidden = []
    for w_ref in (own_ref, other_ref):
        gate = lax.dot_general(
            x, w_ref[0:FF, :], (((1,), (1,)), ((), ())), preferred_element_type=F32
        )
        up = lax.dot_general(
            x, w_ref[FF : 2 * FF, :], (((1,), (1,)), ((), ())), preferred_element_type=F32
        )
        hidden.append((gate / (1.0 + jnp.exp(-gate)) * up).astype(BF16))
    low = lax.broadcasted_iota(jnp.int32, (ROWS, LANES), 1) < 64
    for i in range(4):
        part = 0.0
        for h, w_ref in zip(hidden, (own_ref, other_ref)):
            part = part + jnp.dot(
                h, w_ref[2 * FF : 3 * FF, i * 512 : (i + 1) * 512], preferred_element_type=F32
            )
        part = part * scale
        for b in range(2):
            one = part[:, b * LANES : (b + 1) * LANES]
            two = part[:, (b + 2) * LANES : (b + 3) * LANES]
            mixed = pltpu.roll(jnp.where(low, two, one), 64, 1)
            out_ref[4 * i + 2 * b] = jnp.where(low, one, mixed).astype(BF16)
            out_ref[4 * i + 2 * b + 1] = jnp.where(low, mixed, two).astype(BF16)


def sum_kernel(in_ref, out_ref):
    total = in_ref[0].astype(F32)
    for q in range(1, CHIPS):
        total = total + in_ref[q].astype(F32)
    total = total.reshape(NODES, HALF, LANES)
    turned = pltpu.roll(pltpu.roll(total, 64, 2), 4, 1)
    row = lax.broadcasted_iota(jnp.int32, (NODES, HALF, LANES), 1)
    lane = lax.broadcasted_iota(jnp.int32, (NODES, HALF, LANES), 2)
    out_ref[...] = jnp.where((row < 4) == (lane < 64), total, turned).astype(BF16)


def mix_kernel(in_ref, pos_ref, out_ref):
    tokens = pos_ref.shape[1]
    pos = pos_ref[...]
    row = lax.broadcasted_iota(jnp.int32, (1, HALF, 1), 1)
    values = in_ref[...]
    parts = []
    for h in range(2):
        slot = (row >> 2) * HALF + h * 4 + (row & 3)
        seated = jnp.where(pos[:, None, :] == slot.astype(F32), 1.0, 0.0)
        seated = seated.reshape(ROWS, tokens).astype(BF16)
        parts.append(
            lax.dot_general(
                values, seated, (((0,), (0,)), ((), ())), preferred_element_type=F32
            )
        )
    out_ref[...] = (parts[0][0:64] + parts[1][64:128]).astype(BF16)


def call(kernel, outs, *args, specs=None):
    shapes = [jax.ShapeDtypeStruct(s, d) for s, d in outs]
    many = len(shapes) > 1
    return pl.pallas_call(
        kernel,
        out_shape=shapes if many else shapes[0],
        in_specs=specs or [VMEM] * len(args),
        out_specs=[VMEM] * len(shapes) if many else VMEM,
        compiler_params=PARAMS,
    )(*args)


def per_device(tokens, expert_ids, route_weight, gate_weight, up_weight, down_weight):
    x, core, column = lax.axis_index("x"), lax.axis_index("core"), lax.axis_index("cuts")
    exchange = functools.partial(lax.all_to_all, split_axis=0, concat_axis=0, tiled=True)
    own = jnp.concatenate([gate_weight[0].T, up_weight[0].T, down_weight[0]], axis=0)
    other = lax.ppermute(own, "core", [(0, 1), (1, 0)])

    chip = x * 4 + column
    block = lax.dynamic_slice_in_dim(tokens, chip * LANES, LANES, axis=1)
    where = jnp.stack([core, column]).astype(jnp.int32)
    seats, pos = call(
        seat_kernel,
        [((NODES, 2 * HALF, LANES), BF16), ((NODES, tokens.shape[0]), F32)],
        where,
        expert_ids.T,
        route_weight.T,
        block,
        specs=[SMEM, VMEM, VMEM, VMEM],
    )
    seats = exchange(seats, "node")
    mine = seats[:, :HALF].reshape(1, ROWS, LANES)
    rows = exchange(jnp.broadcast_to(mine, (CHIPS, ROWS, LANES)), ("x", "cuts"))
    parts = call(expert_kernel, [((CHIPS, ROWS, LANES), BF16)], rows, seats, own, other)
    parts = exchange(parts, ("x", "cuts"))
    total = call(sum_kernel, [((NODES, HALF, LANES), BF16)], parts)
    answers = exchange(total.reshape(2 * NODES, HALF // 2, LANES), ("node", "core"))
    mixed = call(mix_kernel, [((64, tokens.shape[0]), BF16)], answers.reshape(ROWS, LANES), pos)
    return mixed.T


def solution(mesh):
    fine = Mesh(mesh.devices.reshape(NODES, 4, 2, 4), ("node", "x", "core", "cuts"))
    in_specs = (
        P("node", None),
        P("node", None),
        P("node", None),
        P(("node", "cuts"), None, ("x", "core")),
        P(("node", "cuts"), None, ("x", "core")),
        P(("node", "cuts"), ("x", "core"), None),
    )
    out_specs = P("node", ("x", "core", "cuts"))
    return jax.shard_map(
        per_device, mesh=fine, in_specs=in_specs, out_specs=out_specs, check_vma=False
    )
```

```python
import functools

import jax
import jax.numpy as jnp
from jax import lax
from jax.experimental import pallas as pl
from jax.experimental.pallas import tpu as pltpu
from jax.sharding import Mesh, PartitionSpec as P

F32 = jnp.float32
BF16 = jnp.bfloat16
NODES = 32
CHIPS = 16
HALF = 8
LANES = 128
WIDTH = 2048
FF = 192
ROWS = NODES * HALF

VMEM = pl.BlockSpec(memory_space=pltpu.VMEM)
SMEM = pl.BlockSpec(memory_space=pltpu.SMEM)
PARAMS = pltpu.CompilerParams(vmem_limit_bytes=16 * 1024 * 1024)


def seat_kernel(where_ref, ids_ref, route_ref, tok_ref, out_ref, scale_ref, pos_ref):
    core = where_ref[0]
    column = where_ref[1]
    tokens = tok_ref.shape[0]
    groups = lax.broadcasted_iota(jnp.int32, (NODES, tokens), 0)
    named = jnp.zeros((NODES, tokens), F32)
    weight = jnp.zeros((NODES, tokens), F32)
    for k in range(ids_ref.shape[0]):
        ids = ids_ref[k : k + 1, :]
        hit = (ids >> 2) == groups
        named = jnp.where(hit, 1.0, named)
        weight = weight + jnp.where(hit & ((ids & 3) == column), route_ref[k : k + 1, :], 0.0)
    before = lax.broadcasted_iota(jnp.int32, (tokens, tokens), 0) < lax.broadcasted_iota(
        jnp.int32, (tokens, tokens), 1
    )
    rank = jnp.dot(named.astype(BF16), before.astype(F32).astype(BF16), preferred_element_type=F32)
    pos = jnp.where(named > 0.0, rank, -1.0)
    pos_ref[...] = pos
    seat = lax.broadcasted_iota(jnp.int32, (1, HALF, 1), 1)
    seated = pos[:, None, :] == (seat + core * HALF).astype(F32)
    rows = jnp.where(seated, 1.0, 0.0).reshape(ROWS, tokens).astype(BF16)
    picked = jnp.dot(rows, tok_ref[...], preferred_element_type=F32)
    out_ref[...] = picked.reshape(NODES, HALF, LANES).astype(BF16)
    scale = jnp.sum(jnp.where(seated, weight[:, None, :], 0.0), axis=2, keepdims=True)
    lane = lax.broadcasted_iota(jnp.int32, (1, 1, LANES), 2)
    scale = jnp.sum(jnp.where(lane == seat, scale, 0.0), axis=1)
    high = scale.astype(BF16)
    scale_ref[0] = high
    scale_ref[1] = (scale - high.astype(F32)).astype(BF16)


def copies_kernel(in_ref, out_ref):
    rows = in_ref[...].reshape(ROWS, LANES)
    for q in range(CHIPS):
        out_ref[q] = rows


def expert_kernel(x_ref, scale_ref, gate0, up0, down0, gate1, up1, down1, out_ref):
    x = jnp.concatenate([x_ref[q] for q in range(CHIPS)], axis=1)
    scale = scale_ref[...]
    lane = lax.broadcasted_iota(jnp.int32, (1, HALF, LANES), 2)
    seat = lax.broadcasted_iota(jnp.int32, (1, HALF, LANES), 1)
    scale = jnp.sum(jnp.where(lane == seat, scale[:, None, :], 0.0), axis=2, keepdims=True)
    scale = scale.reshape(ROWS, 1)
    turned = (((1,), (1,)), ((), ()))
    hidden = []
    for gate_ref, up_ref in ((gate0, up0), (gate1, up1)):
        gate = lax.dot_general(x, gate_ref[...], turned, preferred_element_type=F32)
        up = lax.dot_general(x, up_ref[...], turned, preferred_element_type=F32)
        hidden.append((gate / (1.0 + jnp.exp(-gate)) * up).astype(BF16))
    half = ROWS // 2
    low = lax.broadcasted_iota(jnp.int32, (half, LANES), 1) < 64
    for i in range(8):
        cols = slice(i * 256, (i + 1) * 256)
        part = jnp.dot(hidden[0], down0[:, cols], preferred_element_type=F32) + jnp.dot(hidden[1], down1[:, cols], preferred_element_type=F32)
        part = part * scale
        for b in range(2):
            one = part[:half, b * LANES : (b + 1) * LANES]
            two = part[half:, b * LANES : (b + 1) * LANES]
            mixed = pltpu.roll(jnp.where(low, two, one), 64, 1)
            out_ref[4 * i + 2 * b] = jnp.where(low, one, mixed).astype(BF16)
            out_ref[4 * i + 2 * b + 1] = jnp.where(low, mixed, two).astype(BF16)


def sum_kernel(in_ref, out_ref):
    sums = []
    for core in range(2):
        total = 0.0
        for q in range(CHIPS):
            total = total + in_ref[(q // 4 * 2 + core) * 4 + q % 4].astype(F32)
        sums.append(total)
    one, two = sums
    low = lax.broadcasted_iota(jnp.int32, one.shape, 1) < 64
    mixed = pltpu.roll(jnp.where(low, two, one), 64, 1)
    out_ref[0] = jnp.where(low, one, mixed).astype(BF16)
    out_ref[1] = jnp.where(low, mixed, two).astype(BF16)


def mix_kernel(in_ref, pos_ref, out_ref):
    tokens = pos_ref.shape[1]
    pos = pos_ref[...]
    seat = lax.broadcasted_iota(jnp.int32, (1, HALF, 1), 1)
    values = in_ref[...]
    parts = []
    for core in range(2):
        seated = pos[:, None, :] == (seat + core * HALF).astype(F32)
        seated = jnp.where(seated, 1.0, 0.0).reshape(ROWS, tokens).astype(BF16)
        parts.append(
            lax.dot_general(
                values, seated, (((0,), (0,)), ((), ())), preferred_element_type=F32
            )
        )
    out_ref[...] = (parts[0][0:64] + parts[1][64:128]).astype(BF16)


def call(kernel, outs, *args, specs=None, cost=None):
    shapes = [jax.ShapeDtypeStruct(s, d) for s, d in outs]
    many = len(shapes) > 1
    return pl.pallas_call(
        kernel,
        out_shape=shapes if many else shapes[0],
        in_specs=specs or [VMEM] * len(args),
        out_specs=[VMEM] * len(shapes) if many else VMEM,
        compiler_params=PARAMS,
        cost_estimate=cost,
    )(*args)


def per_device(tokens, expert_ids, route_weight, gate_weight, up_weight, down_weight):
    x, core, column = lax.axis_index("x"), lax.axis_index("core"), lax.axis_index("cuts")
    exchange = functools.partial(lax.all_to_all, split_axis=0, concat_axis=0, tiled=True)
    weights = (gate_weight[0].T, up_weight[0].T, down_weight[0])
    pairs = [(0, 1), (1, 0)]
    weights = weights + tuple(lax.ppermute(w, "core", pairs) for w in weights)
    chip = x * 4 + column
    block = lax.dynamic_slice_in_dim(tokens, chip * LANES, LANES, axis=1)
    where = jnp.stack([core, column]).astype(jnp.int32)
    seats, scale, pos = call(
        seat_kernel,
        [
            ((NODES, HALF, LANES), BF16),
            ((2, NODES, LANES), BF16),
            ((NODES, tokens.shape[0]), F32),
        ],
        where,
        expert_ids.T,
        route_weight.T,
        block,
        specs=[SMEM, VMEM, VMEM, VMEM],
    )
    scale = jnp.swapaxes(scale, 0, 1).reshape(NODES, 1, 2, LANES)
    seats = jnp.concatenate([seats.reshape(NODES, 4, 2, LANES), scale], axis=1)
    seats = exchange(seats, "node")
    scale = seats[:, 4, 0].astype(F32) + seats[:, 4, 1].astype(F32)
    copies = call(
        copies_kernel,
        [((CHIPS, ROWS, LANES), BF16)],
        seats[:, :4].reshape(NODES, HALF, LANES),
        cost=pl.CostEstimate(flops=1 << 20, bytes_accessed=1 << 20, transcendentals=0),
    )
    copies, scale, weights = lax.optimization_barrier((copies, scale, weights))
    rows = exchange(copies, ("x", "cuts"))
    plane = ("x", "core", "cuts")
    parts = call(expert_kernel, [((2 * CHIPS, ROWS // 2, LANES), BF16)], rows, scale, *weights)
    parts = exchange(parts, plane)
    total = call(sum_kernel, [((2, ROWS // 2, LANES), BF16)], parts)
    answers = exchange(total.reshape(NODES, HALF, LANES), "node")
    mixed = call(mix_kernel, [((64, tokens.shape[0]), BF16)], answers.reshape(ROWS, LANES), pos)
    return mixed.T


def solution(mesh):
    fine = Mesh(mesh.devices.reshape(NODES, 4, 2, 4), ("node", "x", "core", "cuts"))
    in_specs = (
        P("node", None),
        P("node", None),
        P("node", None),
        P(("node", "cuts"), None, ("x", "core")),
        P(("node", "cuts"), None, ("x", "core")),
        P(("node", "cuts"), ("x", "core"), None),
    )
    out_specs = P("node", ("x", "core", "cuts"))
    return jax.shard_map(
        per_device, mesh=fine, in_specs=in_specs, out_specs=out_specs, check_vma=False
    )
```

```python
import functools

import jax
import jax.numpy as jnp
from jax import lax
from jax.experimental import pallas as pl
from jax.experimental.pallas import tpu as pltpu
from jax.sharding import Mesh, PartitionSpec as P

F32 = jnp.float32
BF16 = jnp.bfloat16
NODES = 32
CHIPS = 16
HALF = 8
LANES = 128
WIDTH = 2048
FF = 192
ROWS = NODES * HALF

VMEM = pl.BlockSpec(memory_space=pltpu.VMEM)
SMEM = pl.BlockSpec(memory_space=pltpu.SMEM)
PARAMS = pltpu.CompilerParams(vmem_limit_bytes=16 * 1024 * 1024)


def seat_kernel(where_ref, ids_ref, route_ref, tok_ref, out_ref, scale_ref, pos_ref):
    core = where_ref[0]
    column = where_ref[1]
    tokens = tok_ref.shape[0]
    groups = lax.broadcasted_iota(jnp.int32, (NODES, tokens), 0)
    named = jnp.zeros((NODES, tokens), F32)
    weight = jnp.zeros((NODES, tokens), F32)
    for k in range(ids_ref.shape[0]):
        ids = ids_ref[k : k + 1, :]
        hit = (ids >> 2) == groups
        named = jnp.where(hit, 1.0, named)
        weight = weight + jnp.where(hit & ((ids & 3) == column), route_ref[k : k + 1, :], 0.0)
    before = lax.broadcasted_iota(jnp.int32, (tokens, tokens), 0) < lax.broadcasted_iota(
        jnp.int32, (tokens, tokens), 1
    )
    rank = jnp.dot(named.astype(BF16), before.astype(F32).astype(BF16), preferred_element_type=F32)
    pos = jnp.where(named > 0.0, rank, -1.0)
    pos_ref[...] = pos
    seat = lax.broadcasted_iota(jnp.int32, (1, HALF, 1), 1)
    seated = pos[:, None, :] == (seat + core * HALF).astype(F32)
    rows = jnp.where(seated, 1.0, 0.0).reshape(ROWS, tokens).astype(BF16)
    picked = jnp.dot(rows, tok_ref[...], preferred_element_type=F32)
    out_ref[...] = picked.reshape(NODES, HALF, LANES).astype(BF16)
    scale = jnp.sum(jnp.where(seated, weight[:, None, :], 0.0), axis=2, keepdims=True)
    lane = lax.broadcasted_iota(jnp.int32, (1, 1, LANES), 2)
    scale = jnp.sum(jnp.where(lane == seat, scale, 0.0), axis=1)
    high = scale.astype(BF16)
    scale_ref[0] = high
    scale_ref[1] = (scale - high.astype(F32)).astype(BF16)


def copies_kernel(in_ref, out_ref):
    rows = in_ref[...].reshape(ROWS, LANES)
    for q in range(CHIPS):
        out_ref[q] = rows


def expert_kernel(x_ref, scale_ref, gate0, up0, down0, gate1, up1, down1, out_ref):
    x = jnp.concatenate([x_ref[q] for q in range(CHIPS)], axis=1)
    scale = scale_ref[...]
    lane = lax.broadcasted_iota(jnp.int32, (1, HALF, LANES), 2)
    seat = lax.broadcasted_iota(jnp.int32, (1, HALF, LANES), 1)
    scale = jnp.sum(jnp.where(lane == seat, scale[:, None, :], 0.0), axis=2, keepdims=True)
    scale = scale.reshape(ROWS, 1)
    turned = (((1,), (1,)), ((), ()))
    hidden = []
    for gate_ref, up_ref in ((gate0, up0), (gate1, up1)):
        gate = lax.dot_general(x, gate_ref[...], turned, preferred_element_type=F32)
        up = lax.dot_general(x, up_ref[...], turned, preferred_element_type=F32)
        hidden.append((gate / (1.0 + jnp.exp(-gate)) * up).astype(BF16))
    half = ROWS // 2
    low = lax.broadcasted_iota(jnp.int32, (half, LANES), 1) < 64
    for i in range(8):
        cols = slice(i * 256, (i + 1) * 256)
        part = jnp.dot(hidden[0], down0[:, cols], preferred_element_type=F32) + jnp.dot(hidden[1], down1[:, cols], preferred_element_type=F32)
        part = part * scale
        for b in range(2):
            one = part[:half, b * LANES : (b + 1) * LANES]
            two = part[half:, b * LANES : (b + 1) * LANES]
            mixed = pltpu.roll(jnp.where(low, two, one), 64, 1)
            out_ref[4 * i + 2 * b] = jnp.where(low, one, mixed).astype(BF16)
            out_ref[4 * i + 2 * b + 1] = jnp.where(low, mixed, two).astype(BF16)


def sum_kernel(in_ref, out_ref):
    sums = []
    for core in range(2):
        total = 0.0
        for q in range(CHIPS):
            total = total + in_ref[(q // 4 * 2 + core) * 4 + q % 4].astype(F32)
        sums.append(total)
    one, two = sums
    low = lax.broadcasted_iota(jnp.int32, one.shape, 1) < 64
    mixed = pltpu.roll(jnp.where(low, two, one), 64, 1)
    out_ref[0] = jnp.where(low, one, mixed).astype(BF16)
    out_ref[1] = jnp.where(low, mixed, two).astype(BF16)


def mix_kernel(in_ref, pos_ref, out_ref):
    tokens = pos_ref.shape[1]
    pos = pos_ref[...]
    seat = lax.broadcasted_iota(jnp.int32, (1, HALF, 1), 1)
    values = in_ref[...]
    parts = []
    for core in range(2):
        seated = pos[:, None, :] == (seat + core * HALF).astype(F32)
        seated = jnp.where(seated, 1.0, 0.0).reshape(ROWS, tokens).astype(BF16)
        parts.append(
            lax.dot_general(
                values, seated, (((0,), (0,)), ((), ())), preferred_element_type=F32
            )
        )
    out_ref[...] = (parts[0][0:64] + parts[1][64:128]).astype(BF16)


def call(kernel, outs, *args, specs=None, cost=None):
    shapes = [jax.ShapeDtypeStruct(s, d) for s, d in outs]
    many = len(shapes) > 1
    return pl.pallas_call(
        kernel,
        out_shape=shapes if many else shapes[0],
        in_specs=specs or [VMEM] * len(args),
        out_specs=[VMEM] * len(shapes) if many else VMEM,
        compiler_params=PARAMS,
        cost_estimate=cost,
    )(*args)


def per_device(tokens, expert_ids, route_weight, gate_weight, up_weight, down_weight):
    x, core, column = lax.axis_index("x"), lax.axis_index("core"), lax.axis_index("cuts")
    exchange = functools.partial(lax.all_to_all, split_axis=0, concat_axis=0, tiled=True)
    weights = (gate_weight[0].T, up_weight[0].T, down_weight[0])
    pairs = [(0, 1), (1, 0)]
    weights = weights + tuple(lax.ppermute(w, "core", pairs) for w in weights)
    chip = column * 4 + x
    block = lax.dynamic_slice_in_dim(tokens, chip * LANES, LANES, axis=1)
    where = jnp.stack([core, column]).astype(jnp.int32)
    seats, scale, pos = call(
        seat_kernel,
        [
            ((NODES, HALF, LANES), BF16),
            ((2, NODES, LANES), BF16),
            ((NODES, tokens.shape[0]), F32),
        ],
        where,
        expert_ids.T,
        route_weight.T,
        block,
        specs=[SMEM, VMEM, VMEM, VMEM],
    )
    scale = jnp.swapaxes(scale, 0, 1).reshape(NODES, 1, 2, LANES)
    seats = jnp.concatenate([seats.reshape(NODES, 4, 2, LANES), scale], axis=1)
    seats = exchange(seats, "node")
    scale = seats[:, 4, 0].astype(F32) + seats[:, 4, 1].astype(F32)
    copies = call(
        copies_kernel,
        [((CHIPS, ROWS, LANES), BF16)],
        seats[:, :4].reshape(NODES, HALF, LANES),
        cost=pl.CostEstimate(flops=1 << 20, bytes_accessed=1 << 20, transcendentals=0),
    )
    copies, scale, weights = lax.optimization_barrier((copies, scale, weights))
    rows = exchange(copies, ("cuts", "x"))
    plane = ("x", "core", "cuts")
    parts = call(expert_kernel, [((2 * CHIPS, ROWS // 2, LANES), BF16)], rows, scale, *weights)
    parts = exchange(parts, plane)
    total = call(sum_kernel, [((2, ROWS // 2, LANES), BF16)], parts)
    answers = exchange(total.reshape(NODES, HALF, LANES), "node")
    mixed = call(mix_kernel, [((64, tokens.shape[0]), BF16)], answers.reshape(ROWS, LANES), pos)
    return mixed.T


def solution(mesh):
    fine = Mesh(mesh.devices.reshape(NODES, 4, 2, 4), ("node", "x", "core", "cuts"))
    in_specs = (
        P("node", None),
        P("node", None),
        P("node", None),
        P(("node", "cuts"), None, ("x", "core")),
        P(("node", "cuts"), None, ("x", "core")),
        P(("node", "cuts"), ("x", "core"), None),
    )
    out_specs = P("node", ("x", "core", "cuts"))
    return jax.shard_map(
        per_device, mesh=fine, in_specs=in_specs, out_specs=out_specs, check_vma=False
    )
```

```python
import functools

import jax
import jax.numpy as jnp
from jax import lax
from jax.experimental import pallas as pl
from jax.experimental.pallas import tpu as pltpu
from jax.sharding import Mesh, PartitionSpec as P

F32 = jnp.float32
BF16 = jnp.bfloat16
NODES = 32
FIRST = 16
CHIPS = 16
HALF = 8
LANES = 128
WIDTH = 2048
FF = 192
ROWS = NODES * HALF

VMEM = pl.BlockSpec(memory_space=pltpu.VMEM)
SMEM = pl.BlockSpec(memory_space=pltpu.SMEM)
PARAMS = pltpu.CompilerParams(vmem_limit_bytes=16 * 1024 * 1024)


def seat_kernel(where_ref, ids_ref, route_ref, tok_ref, out_ref, scale_ref, pos_ref):
    core = where_ref[0]
    column = where_ref[1]
    tokens = tok_ref.shape[0]
    groups = (lax.broadcasted_iota(jnp.int32, (NODES, tokens), 0) + FIRST) & (NODES - 1)
    named = jnp.zeros((NODES, tokens), F32)
    weight = jnp.zeros((NODES, tokens), F32)
    for k in range(ids_ref.shape[0]):
        ids = ids_ref[k : k + 1, :]
        hit = (ids >> 2) == groups
        named = jnp.where(hit, 1.0, named)
        weight = weight + jnp.where(hit & ((ids & 3) == column), route_ref[k : k + 1, :], 0.0)
    before = lax.broadcasted_iota(jnp.int32, (tokens, tokens), 0) < lax.broadcasted_iota(
        jnp.int32, (tokens, tokens), 1
    )
    rank = jnp.dot(named.astype(BF16), before.astype(F32).astype(BF16), preferred_element_type=F32)
    pos = jnp.where(named > 0.0, rank, -1.0)
    pos_ref[...] = pos
    seat = lax.broadcasted_iota(jnp.int32, (1, HALF, 1), 1)
    seated = pos[:, None, :] == (seat + core * HALF).astype(F32)
    rows = jnp.where(seated, 1.0, 0.0).reshape(ROWS, tokens).astype(BF16)
    picked = jnp.dot(rows, tok_ref[...], preferred_element_type=F32)
    out_ref[...] = picked.reshape(NODES, HALF, LANES).astype(BF16)
    scale = jnp.sum(jnp.where(seated, weight[:, None, :], 0.0), axis=2, keepdims=True)
    lane = lax.broadcasted_iota(jnp.int32, (1, 1, LANES), 2)
    scale = jnp.sum(jnp.where(lane == seat, scale, 0.0), axis=1)
    high = scale.astype(BF16)
    scale_ref[0] = high
    scale_ref[1] = (scale - high.astype(F32)).astype(BF16)


def copies_kernel(in_ref, out_ref):
    rows = in_ref[...].reshape(ROWS, LANES)
    for q in range(CHIPS):
        out_ref[q] = rows


def expert_kernel(x_ref, scale_ref, gate0, up0, down0, gate1, up1, down1, out_ref):
    x = jnp.concatenate([x_ref[q] for q in range(CHIPS)], axis=1)
    scale = scale_ref[...]
    lane = lax.broadcasted_iota(jnp.int32, (1, HALF, LANES), 2)
    seat = lax.broadcasted_iota(jnp.int32, (1, HALF, LANES), 1)
    scale = jnp.sum(jnp.where(lane == seat, scale[:, None, :], 0.0), axis=2, keepdims=True)
    scale = scale.reshape(ROWS, 1)
    turned = (((1,), (1,)), ((), ()))
    hidden = []
    for gate_ref, up_ref in ((gate0, up0), (gate1, up1)):
        gate = lax.dot_general(x, gate_ref[...], turned, preferred_element_type=F32)
        up = lax.dot_general(x, up_ref[...], turned, preferred_element_type=F32)
        hidden.append((gate / (1.0 + jnp.exp(-gate)) * up).astype(BF16))
    half = ROWS // 2
    low = lax.broadcasted_iota(jnp.int32, (half, LANES), 1) < 64
    for i in range(8):
        cols = slice(i * 256, (i + 1) * 256)
        part = jnp.dot(hidden[0], down0[:, cols], preferred_element_type=F32) + jnp.dot(hidden[1], down1[:, cols], preferred_element_type=F32)
        part = part * scale
        for b in range(2):
            one = part[:half, b * LANES : (b + 1) * LANES]
            two = part[half:, b * LANES : (b + 1) * LANES]
            mixed = pltpu.roll(jnp.where(low, two, one), 64, 1)
            out_ref[4 * i + 2 * b] = jnp.where(low, one, mixed).astype(BF16)
            out_ref[4 * i + 2 * b + 1] = jnp.where(low, mixed, two).astype(BF16)


def sum_kernel(in_ref, out_ref):
    sums = []
    for core in range(2):
        total = 0.0
        for q in range(CHIPS):
            total = total + in_ref[(q // 4 * 2 + core) * 4 + q % 4].astype(F32)
        sums.append(total)
    one, two = sums
    low = lax.broadcasted_iota(jnp.int32, one.shape, 1) < 64
    mixed = pltpu.roll(jnp.where(low, two, one), 64, 1)
    out_ref[0] = jnp.where(low, one, mixed).astype(BF16)
    out_ref[1] = jnp.where(low, mixed, two).astype(BF16)


def mix_kernel(in_ref, pos_ref, out_ref):
    tokens = pos_ref.shape[1]
    pos = pos_ref[...]
    seat = lax.broadcasted_iota(jnp.int32, (1, HALF, 1), 1)
    values = in_ref[...]
    parts = []
    for core in range(2):
        seated = pos[:, None, :] == (seat + core * HALF).astype(F32)
        seated = jnp.where(seated, 1.0, 0.0).reshape(ROWS, tokens).astype(BF16)
        parts.append(
            lax.dot_general(
                values, seated, (((0,), (0,)), ((), ())), preferred_element_type=F32
            )
        )
    out_ref[...] = (parts[0][0:64] + parts[1][64:128]).astype(BF16)


def call(kernel, outs, *args, specs=None, cost=None):
    shapes = [jax.ShapeDtypeStruct(s, d) for s, d in outs]
    many = len(shapes) > 1
    return pl.pallas_call(
        kernel,
        out_shape=shapes if many else shapes[0],
        in_specs=specs or [VMEM] * len(args),
        out_specs=[VMEM] * len(shapes) if many else VMEM,
        compiler_params=PARAMS,
        cost_estimate=cost,
    )(*args)


def per_device(tokens, expert_ids, route_weight, gate_weight, up_weight, down_weight):
    x, core, column = lax.axis_index("x"), lax.axis_index("core"), lax.axis_index("cuts")
    exchange = functools.partial(lax.all_to_all, split_axis=0, concat_axis=0, tiled=True)
    ring = [[(FIRST + i) % NODES for i in range(NODES)]]
    weights = (gate_weight[0].T, up_weight[0].T, down_weight[0])
    pairs = [(0, 1), (1, 0)]
    weights = weights + tuple(lax.ppermute(w, "core", pairs) for w in weights)
    chip = column * 4 + x
    block = lax.dynamic_slice_in_dim(tokens, chip * LANES, LANES, axis=1)
    where = jnp.stack([core, column]).astype(jnp.int32)
    seats, scale, pos = call(
        seat_kernel,
        [
            ((NODES, HALF, LANES), BF16),
            ((2, NODES, LANES), BF16),
            ((NODES, tokens.shape[0]), F32),
        ],
        where,
        expert_ids.T,
        route_weight.T,
        block,
        specs=[SMEM, VMEM, VMEM, VMEM],
    )
    scale = jnp.swapaxes(scale, 0, 1).reshape(NODES, 1, 2, LANES)
    seats = jnp.concatenate([seats.reshape(NODES, 4, 2, LANES), scale], axis=1)
    seats = exchange(seats, "node", axis_index_groups=ring)
    scale = seats[:, 4, 0].astype(F32) + seats[:, 4, 1].astype(F32)
    copies = call(
        copies_kernel,
        [((CHIPS, ROWS, LANES), BF16)],
        seats[:, :4].reshape(NODES, HALF, LANES),
        cost=pl.CostEstimate(flops=1 << 20, bytes_accessed=1 << 20, transcendentals=0),
    )
    copies, scale, weights = lax.optimization_barrier((copies, scale, weights))
    rows = exchange(copies, ("cuts", "x"))
    plane = ("x", "core", "cuts")
    parts = call(expert_kernel, [((2 * CHIPS, ROWS // 2, LANES), BF16)], rows, scale, *weights)
    parts = exchange(parts, plane)
    total = call(sum_kernel, [((2, ROWS // 2, LANES), BF16)], parts)
    answers = exchange(total.reshape(NODES, HALF, LANES), "node", axis_index_groups=ring)
    mixed = call(mix_kernel, [((64, tokens.shape[0]), BF16)], answers.reshape(ROWS, LANES), pos)
    return mixed.T


def solution(mesh):
    fine = Mesh(mesh.devices.reshape(NODES, 4, 2, 4), ("node", "x", "core", "cuts"))
    in_specs = (
        P("node", None),
        P("node", None),
        P("node", None),
        P(("node", "cuts"), None, ("x", "core")),
        P(("node", "cuts"), None, ("x", "core")),
        P(("node", "cuts"), ("x", "core"), None),
    )
    out_specs = P("node", ("x", "core", "cuts"))
    return jax.shard_map(
        per_device, mesh=fine, in_specs=in_specs, out_specs=out_specs, check_vma=False
    )
```

```python
import functools

import jax
import jax.numpy as jnp
from jax import lax
from jax.experimental import pallas as pl
from jax.experimental.pallas import tpu as pltpu
from jax.sharding import Mesh, PartitionSpec as P

F32 = jnp.float32
BF16 = jnp.bfloat16
NODES = 32
FIRST = 20
BACK = 16
TURN = FIRST - BACK
CHIPS = 16
HALF = 8
LANES = 128
WIDTH = 2048
FF = 192
ROWS = NODES * HALF

VMEM = pl.BlockSpec(memory_space=pltpu.VMEM)
SMEM = pl.BlockSpec(memory_space=pltpu.SMEM)
PARAMS = pltpu.CompilerParams(vmem_limit_bytes=16 * 1024 * 1024)


def seat_kernel(where_ref, ids_ref, route_ref, tok_ref, out_ref, scale_ref, pos_ref):
    core = where_ref[0]
    column = where_ref[1]
    tokens = tok_ref.shape[0]
    groups = (lax.broadcasted_iota(jnp.int32, (NODES, tokens), 0) + FIRST) & (NODES - 1)
    named = jnp.zeros((NODES, tokens), F32)
    weight = jnp.zeros((NODES, tokens), F32)
    for k in range(ids_ref.shape[0]):
        ids = ids_ref[k : k + 1, :]
        hit = (ids >> 2) == groups
        named = jnp.where(hit, 1.0, named)
        weight = weight + jnp.where(hit & ((ids & 3) == column), route_ref[k : k + 1, :], 0.0)
    before = lax.broadcasted_iota(jnp.int32, (tokens, tokens), 0) < lax.broadcasted_iota(
        jnp.int32, (tokens, tokens), 1
    )
    rank = jnp.dot(named.astype(BF16), before.astype(F32).astype(BF16), preferred_element_type=F32)
    pos = jnp.where(named > 0.0, rank, -1.0)
    pos_ref[...] = pltpu.roll(pos, TURN, 0)
    seat = lax.broadcasted_iota(jnp.int32, (1, HALF, 1), 1)
    seated = pos[:, None, :] == (seat + core * HALF).astype(F32)
    rows = jnp.where(seated, 1.0, 0.0).reshape(ROWS, tokens).astype(BF16)
    picked = jnp.dot(rows, tok_ref[...], preferred_element_type=F32)
    out_ref[...] = picked.reshape(NODES, HALF, LANES).astype(BF16)
    scale = jnp.sum(jnp.where(seated, weight[:, None, :], 0.0), axis=2, keepdims=True)
    lane = lax.broadcasted_iota(jnp.int32, (1, 1, LANES), 2)
    scale = jnp.sum(jnp.where(lane == seat, scale, 0.0), axis=1)
    high = scale.astype(BF16)
    scale_ref[0] = high
    scale_ref[1] = (scale - high.astype(F32)).astype(BF16)


def copies_kernel(in_ref, out_ref):
    rows = in_ref[...].reshape(ROWS, LANES)
    for q in range(CHIPS):
        out_ref[q] = rows


def expert_kernel(x_ref, scale_ref, gate0, up0, down0, gate1, up1, down1, out_ref):
    x = jnp.concatenate([x_ref[q] for q in range(CHIPS)], axis=1)
    scale = scale_ref[...]
    lane = lax.broadcasted_iota(jnp.int32, (1, HALF, LANES), 2)
    seat = lax.broadcasted_iota(jnp.int32, (1, HALF, LANES), 1)
    scale = jnp.sum(jnp.where(lane == seat, scale[:, None, :], 0.0), axis=2, keepdims=True)
    scale = scale.reshape(ROWS, 1)
    turned = (((1,), (1,)), ((), ()))
    hidden = []
    for gate_ref, up_ref in ((gate0, up0), (gate1, up1)):
        gate = lax.dot_general(x, gate_ref[...], turned, preferred_element_type=F32)
        up = lax.dot_general(x, up_ref[...], turned, preferred_element_type=F32)
        hidden.append((gate / (1.0 + jnp.exp(-gate)) * up).astype(BF16))
    half = ROWS // 2
    low = lax.broadcasted_iota(jnp.int32, (half, LANES), 1) < 64
    for i in range(8):
        cols = slice(i * 256, (i + 1) * 256)
        part = jnp.dot(hidden[0], down0[:, cols], preferred_element_type=F32) + jnp.dot(hidden[1], down1[:, cols], preferred_element_type=F32)
        part = part * scale
        for b in range(2):
            one = part[:half, b * LANES : (b + 1) * LANES]
            two = part[half:, b * LANES : (b + 1) * LANES]
            mixed = pltpu.roll(jnp.where(low, two, one), 64, 1)
            out_ref[4 * i + 2 * b] = jnp.where(low, one, mixed).astype(BF16)
            out_ref[4 * i + 2 * b + 1] = jnp.where(low, mixed, two).astype(BF16)


def sum_kernel(in_ref, out_ref):
    sums = []
    for core in range(2):
        total = 0.0
        for q in range(CHIPS):
            total = total + in_ref[(q // 4 * 2 + core) * 4 + q % 4].astype(F32)
        sums.append(total)
    one, two = sums
    low = lax.broadcasted_iota(jnp.int32, one.shape, 1) < 64
    mixed = pltpu.roll(jnp.where(low, two, one), 64, 1)
    rows = (jnp.where(low, one, mixed).astype(BF16), jnp.where(low, mixed, two).astype(BF16))
    turn, stay = TURN * HALF, rows[0].shape[0] - TURN * HALF
    for half in range(2):
        out_ref[half, turn:] = rows[half][:stay]
        out_ref[1 - half, :turn] = rows[half][stay:]


def mix_kernel(in_ref, pos_ref, out_ref):
    tokens = pos_ref.shape[1]
    pos = pos_ref[...]
    seat = lax.broadcasted_iota(jnp.int32, (1, HALF, 1), 1)
    values = in_ref[...]
    parts = []
    for core in range(2):
        seated = pos[:, None, :] == (seat + core * HALF).astype(F32)
        seated = jnp.where(seated, 1.0, 0.0).reshape(ROWS, tokens).astype(BF16)
        parts.append(
            lax.dot_general(
                values, seated, (((0,), (0,)), ((), ())), preferred_element_type=F32
            )
        )
    out_ref[...] = (parts[0][0:64] + parts[1][64:128]).astype(BF16)


def call(kernel, outs, *args, specs=None, cost=None):
    shapes = [jax.ShapeDtypeStruct(s, d) for s, d in outs]
    many = len(shapes) > 1
    return pl.pallas_call(
        kernel,
        out_shape=shapes if many else shapes[0],
        in_specs=specs or [VMEM] * len(args),
        out_specs=[VMEM] * len(shapes) if many else VMEM,
        compiler_params=PARAMS,
        cost_estimate=cost,
    )(*args)


def per_device(tokens, expert_ids, route_weight, gate_weight, up_weight, down_weight):
    x, core, column = lax.axis_index("x"), lax.axis_index("core"), lax.axis_index("cuts")
    exchange = functools.partial(lax.all_to_all, split_axis=0, concat_axis=0, tiled=True)
    out_ring = [[(FIRST + i) % NODES for i in range(NODES)]]
    back_ring = [[(BACK + i) % NODES for i in range(NODES)]]
    weights = (gate_weight[0].T, up_weight[0].T, down_weight[0])
    pairs = [(0, 1), (1, 0)]
    weights = weights + tuple(lax.ppermute(w, "core", pairs) for w in weights)
    chip = column * 4 + x
    block = lax.dynamic_slice_in_dim(tokens, chip * LANES, LANES, axis=1)
    where = jnp.stack([core, column]).astype(jnp.int32)
    seats, scale, pos = call(
        seat_kernel,
        [
            ((NODES, HALF, LANES), BF16),
            ((2, NODES, LANES), BF16),
            ((NODES, tokens.shape[0]), F32),
        ],
        where,
        expert_ids.T,
        route_weight.T,
        block,
        specs=[SMEM, VMEM, VMEM, VMEM],
    )
    scale = jnp.swapaxes(scale, 0, 1).reshape(NODES, 1, 2, LANES)
    seats = jnp.concatenate([seats.reshape(NODES, 4, 2, LANES), scale], axis=1)
    seats = exchange(seats, "node", axis_index_groups=out_ring)
    scale = seats[:, 4, 0].astype(F32) + seats[:, 4, 1].astype(F32)
    copies = call(
        copies_kernel,
        [((CHIPS, ROWS, LANES), BF16)],
        seats[:, :4].reshape(NODES, HALF, LANES),
        cost=pl.CostEstimate(flops=1 << 20, bytes_accessed=1 << 20, transcendentals=0),
    )
    copies, scale, weights = lax.optimization_barrier((copies, scale, weights))
    rows = exchange(copies, ("cuts", "x"))
    plane = ("x", "core", "cuts")
    parts = call(expert_kernel, [((2 * CHIPS, ROWS // 2, LANES), BF16)], rows, scale, *weights)
    parts = exchange(parts, plane)
    total = call(sum_kernel, [((2, ROWS // 2, LANES), BF16)], parts)
    answers = exchange(
        total.reshape(NODES, HALF, LANES), "node", axis_index_groups=back_ring
    )
    mixed = call(mix_kernel, [((64, tokens.shape[0]), BF16)], answers.reshape(ROWS, LANES), pos)
    return mixed.T


def solution(mesh):
    fine = Mesh(mesh.devices.reshape(NODES, 4, 2, 4), ("node", "x", "core", "cuts"))
    in_specs = (
        P("node", None),
        P("node", None),
        P("node", None),
        P(("node", "cuts"), None, ("x", "core")),
        P(("node", "cuts"), None, ("x", "core")),
        P(("node", "cuts"), ("x", "core"), None),
    )
    out_specs = P("node", ("x", "core", "cuts"))
    return jax.shard_map(
        per_device, mesh=fine, in_specs=in_specs, out_specs=out_specs, check_vma=False
    )
```

```python
import functools

import jax
import jax.numpy as jnp
from jax import lax
from jax.experimental import pallas as pl
from jax.experimental.pallas import tpu as pltpu
from jax.sharding import Mesh, PartitionSpec as P

F32 = jnp.float32
BF16 = jnp.bfloat16
NODES = 32
FIRST = 20
BACK = 16
TURN = FIRST - BACK
CHIPS = 16
HALF = 8
LANES = 128
WIDTH = 2048
FF = 192
ROWS = NODES * HALF

VMEM = pl.BlockSpec(memory_space=pltpu.VMEM)
SMEM = pl.BlockSpec(memory_space=pltpu.SMEM)
PARAMS = pltpu.CompilerParams(vmem_limit_bytes=16 * 1024 * 1024)


def seat_kernel(where_ref, ids_ref, route_ref, out_ref, scale_ref, pos_ref):
    core = where_ref[0]
    column = where_ref[1]
    tokens = ids_ref.shape[1]
    groups = (lax.broadcasted_iota(jnp.int32, (NODES, tokens), 0) + FIRST) & (NODES - 1)
    named = jnp.zeros((NODES, tokens), F32)
    weight = jnp.zeros((NODES, tokens), F32)
    for k in range(ids_ref.shape[0]):
        ids = ids_ref[k : k + 1, :]
        hit = (ids >> 2) == groups
        named = jnp.where(hit, 1.0, named)
        weight = weight + jnp.where(hit & ((ids & 3) == column), route_ref[k : k + 1, :], 0.0)
    before = lax.broadcasted_iota(jnp.int32, (tokens, tokens), 0) < lax.broadcasted_iota(
        jnp.int32, (tokens, tokens), 1
    )
    rank = jnp.dot(named.astype(BF16), before.astype(F32).astype(BF16), preferred_element_type=F32)
    pos = jnp.where(named > 0.0, rank, -1.0)
    pos_ref[...] = pltpu.roll(pos, TURN, 0)
    seat = lax.broadcasted_iota(jnp.int32, (1, HALF, 1), 1)
    seated = pos[:, None, :] == (seat + core * HALF).astype(F32)
    rows = jnp.where(seated, 1.0, 0.0).reshape(ROWS, tokens).astype(BF16)
    out_ref[...] = rows
    scale = jnp.sum(jnp.where(seated, weight[:, None, :], 0.0), axis=2, keepdims=True)
    lane = lax.broadcasted_iota(jnp.int32, (1, 1, LANES), 2)
    scale = jnp.sum(jnp.where(lane == seat, scale, 0.0), axis=1)
    high = scale.astype(BF16)
    scale_ref[0] = high
    scale_ref[1] = (scale - high.astype(F32)).astype(BF16)


def pick_kernel(rows_ref, tok_ref, out_ref):
    picked = jnp.dot(rows_ref[...], tok_ref[...], preferred_element_type=F32)
    out_ref[...] = picked.reshape(NODES, HALF, LANES).astype(BF16)


def copies_kernel(in_ref, out_ref):
    rows = in_ref[...].reshape(ROWS, LANES)
    for q in range(CHIPS):
        out_ref[q] = rows


def expert_kernel(x_ref, scale_ref, gate0, up0, down0, gate1, up1, down1, out_ref):
    x = jnp.concatenate([x_ref[q] for q in range(CHIPS)], axis=1)
    scale = scale_ref[...]
    lane = lax.broadcasted_iota(jnp.int32, (1, HALF, LANES), 2)
    seat = lax.broadcasted_iota(jnp.int32, (1, HALF, LANES), 1)
    scale = jnp.sum(jnp.where(lane == seat, scale[:, None, :], 0.0), axis=2, keepdims=True)
    scale = scale.reshape(ROWS, 1)
    turned = (((1,), (1,)), ((), ()))
    hidden = []
    for gate_ref, up_ref in ((gate0, up0), (gate1, up1)):
        gate = lax.dot_general(x, gate_ref[...], turned, preferred_element_type=F32)
        up = lax.dot_general(x, up_ref[...], turned, preferred_element_type=F32)
        hidden.append((gate / (1.0 + jnp.exp(-gate)) * up).astype(BF16))
    half = ROWS // 2
    low = lax.broadcasted_iota(jnp.int32, (half, LANES), 1) < 64
    for i in range(8):
        cols = slice(i * 256, (i + 1) * 256)
        part = jnp.dot(hidden[0], down0[:, cols], preferred_element_type=F32) + jnp.dot(hidden[1], down1[:, cols], preferred_element_type=F32)
        part = part * scale
        for b in range(2):
            one = part[:half, b * LANES : (b + 1) * LANES]
            two = part[half:, b * LANES : (b + 1) * LANES]
            mixed = pltpu.roll(jnp.where(low, two, one), 64, 1)
            out_ref[4 * i + 2 * b] = jnp.where(low, one, mixed).astype(BF16)
            out_ref[4 * i + 2 * b + 1] = jnp.where(low, mixed, two).astype(BF16)


def sum_kernel(in_ref, out_ref):
    sums = []
    for core in range(2):
        total = 0.0
        for q in range(CHIPS):
            total = total + in_ref[(q // 4 * 2 + core) * 4 + q % 4].astype(F32)
        sums.append(total)
    one, two = sums
    low = lax.broadcasted_iota(jnp.int32, one.shape, 1) < 64
    mixed = pltpu.roll(jnp.where(low, two, one), 64, 1)
    rows = (jnp.where(low, one, mixed).astype(BF16), jnp.where(low, mixed, two).astype(BF16))
    turn, stay = TURN * HALF, rows[0].shape[0] - TURN * HALF
    for half in range(2):
        out_ref[half, turn:] = rows[half][:stay]
        out_ref[1 - half, :turn] = rows[half][stay:]


def mix_kernel(in_ref, pos_ref, out_ref):
    tokens = pos_ref.shape[1]
    pos = pos_ref[...]
    seat = lax.broadcasted_iota(jnp.int32, (1, HALF, 1), 1)
    values = in_ref[...]
    parts = []
    for core in range(2):
        seated = pos[:, None, :] == (seat + core * HALF).astype(F32)
        seated = jnp.where(seated, 1.0, 0.0).reshape(ROWS, tokens).astype(BF16)
        parts.append(
            lax.dot_general(
                values, seated, (((0,), (0,)), ((), ())), preferred_element_type=F32
            )
        )
    out_ref[...] = (parts[0][0:64] + parts[1][64:128]).astype(BF16)


def call(kernel, outs, *args, specs=None, cost=None):
    shapes = [jax.ShapeDtypeStruct(s, d) for s, d in outs]
    many = len(shapes) > 1
    return pl.pallas_call(
        kernel,
        out_shape=shapes if many else shapes[0],
        in_specs=specs or [VMEM] * len(args),
        out_specs=[VMEM] * len(shapes) if many else VMEM,
        compiler_params=PARAMS,
        cost_estimate=cost,
    )(*args)


def per_device(tokens, expert_ids, route_weight, gate_weight, up_weight, down_weight):
    x, core, column = lax.axis_index("x"), lax.axis_index("core"), lax.axis_index("cuts")
    exchange = functools.partial(lax.all_to_all, split_axis=0, concat_axis=0, tiled=True)
    out_ring = [[(FIRST + i) % NODES for i in range(NODES)]]
    back_ring = [[(BACK + i) % NODES for i in range(NODES)]]
    weights = (gate_weight[0].T, up_weight[0].T, down_weight[0])
    pairs = [(0, 1), (1, 0)]
    weights = weights + tuple(lax.ppermute(w, "core", pairs) for w in weights)
    chip = column * 4 + x
    block = lax.dynamic_slice_in_dim(tokens, chip * LANES, LANES, axis=1)
    where = jnp.stack([core, column]).astype(jnp.int32)
    seats, scale, pos = call(
        seat_kernel,
        [
            ((ROWS, tokens.shape[0]), BF16),
            ((2, NODES, LANES), BF16),
            ((NODES, tokens.shape[0]), F32),
        ],
        where,
        expert_ids.T,
        route_weight.T,
        specs=[SMEM, VMEM, VMEM],
    )
    seats = call(pick_kernel, [((NODES, HALF, LANES), BF16)], seats, block)
    scale = jnp.swapaxes(scale, 0, 1).reshape(NODES, 1, 2, LANES)
    seats = jnp.concatenate([seats.reshape(NODES, 4, 2, LANES), scale], axis=1)
    seats = exchange(seats, "node", axis_index_groups=out_ring)
    scale = seats[:, 4, 0].astype(F32) + seats[:, 4, 1].astype(F32)
    copies = call(
        copies_kernel,
        [((CHIPS, ROWS, LANES), BF16)],
        seats[:, :4].reshape(NODES, HALF, LANES),
        cost=pl.CostEstimate(flops=1 << 20, bytes_accessed=1 << 20, transcendentals=0),
    )
    copies, scale, weights = lax.optimization_barrier((copies, scale, weights))
    rows = exchange(copies, ("cuts", "x"))
    plane = ("x", "core", "cuts")
    parts = call(expert_kernel, [((2 * CHIPS, ROWS // 2, LANES), BF16)], rows, scale, *weights)
    parts = exchange(parts, plane)
    total = call(sum_kernel, [((2, ROWS // 2, LANES), BF16)], parts)
    answers = exchange(
        total.reshape(NODES, HALF, LANES), "node", axis_index_groups=back_ring
    )
    mixed = call(mix_kernel, [((64, tokens.shape[0]), BF16)], answers.reshape(ROWS, LANES), pos)
    return mixed.T


def solution(mesh):
    fine = Mesh(mesh.devices.reshape(NODES, 4, 2, 4), ("node", "x", "core", "cuts"))
    in_specs = (
        P("node", None),
        P("node", None),
        P("node", None),
        P(("node", "cuts"), None, ("x", "core")),
        P(("node", "cuts"), None, ("x", "core")),
        P(("node", "cuts"), ("x", "core"), None),
    )
    out_specs = P("node", ("x", "core", "cuts"))
    return jax.shard_map(
        per_device, mesh=fine, in_specs=in_specs, out_specs=out_specs, check_vma=False
    )
```

```python
import functools

import jax
import jax.numpy as jnp
from jax import lax
from jax.experimental import pallas as pl
from jax.experimental.pallas import tpu as pltpu
from jax.sharding import Mesh, PartitionSpec as P

F32 = jnp.float32
BF16 = jnp.bfloat16
NODES = 32
FIRST = 18
BACK = 16
TURN = FIRST - BACK
CHIPS = 16
HALF = 8
LANES = 128
WIDTH = 2048
FF = 192
ROWS = NODES * HALF

VMEM = pl.BlockSpec(memory_space=pltpu.VMEM)
SMEM = pl.BlockSpec(memory_space=pltpu.SMEM)
PARAMS = pltpu.CompilerParams(vmem_limit_bytes=16 * 1024 * 1024)


def seat_kernel(where_ref, ids_ref, route_ref, out_ref, scale_ref, pos_ref):
    core = where_ref[0]
    column = where_ref[1]
    tokens = ids_ref.shape[1]
    groups = (lax.broadcasted_iota(jnp.int32, (NODES, tokens), 0) + FIRST) & (NODES - 1)
    named = jnp.zeros((NODES, tokens), F32)
    weight = jnp.zeros((NODES, tokens), F32)
    for k in range(ids_ref.shape[0]):
        ids = ids_ref[k : k + 1, :]
        hit = (ids >> 2) == groups
        named = jnp.where(hit, 1.0, named)
        weight = weight + jnp.where(hit & ((ids & 3) == column), route_ref[k : k + 1, :], 0.0)
    before = lax.broadcasted_iota(jnp.int32, (tokens, tokens), 0) < lax.broadcasted_iota(
        jnp.int32, (tokens, tokens), 1
    )
    rank = jnp.dot(named.astype(BF16), before.astype(F32).astype(BF16), preferred_element_type=F32)
    pos = jnp.where(named > 0.0, rank, -1.0)
    pos_ref[...] = pltpu.roll(pos, TURN, 0)
    seat = lax.broadcasted_iota(jnp.int32, (1, HALF, 1), 1)
    seated = pos[:, None, :] == (seat + core * HALF).astype(F32)
    rows = jnp.where(seated, 1.0, 0.0).reshape(ROWS, tokens).astype(BF16)
    out_ref[...] = rows
    scale = jnp.sum(jnp.where(seated, weight[:, None, :], 0.0), axis=2, keepdims=True)
    lane = lax.broadcasted_iota(jnp.int32, (1, 1, LANES), 2)
    scale = jnp.sum(jnp.where(lane == seat, scale, 0.0), axis=1)
    high = scale.astype(BF16)
    scale_ref[0] = high
    scale_ref[1] = (scale - high.astype(F32)).astype(BF16)


def pick_kernel(rows_ref, tok_ref, out_ref):
    picked = jnp.dot(rows_ref[...], tok_ref[...], preferred_element_type=F32)
    out_ref[...] = picked.reshape(NODES, HALF, LANES).astype(BF16)


def copies_kernel(in_ref, out_ref):
    rows = in_ref[...].reshape(ROWS, LANES)
    for q in range(CHIPS):
        out_ref[q] = rows


def expert_kernel(x_ref, scale_ref, gate0, up0, down0, gate1, up1, down1, out_ref):
    x = jnp.concatenate([x_ref[q] for q in range(CHIPS)], axis=1)
    scale = scale_ref[...]
    lane = lax.broadcasted_iota(jnp.int32, (1, HALF, LANES), 2)
    seat = lax.broadcasted_iota(jnp.int32, (1, HALF, LANES), 1)
    scale = jnp.sum(jnp.where(lane == seat, scale[:, None, :], 0.0), axis=2, keepdims=True)
    scale = scale.reshape(ROWS, 1)
    turned = (((1,), (1,)), ((), ()))
    hidden = []
    for gate_ref, up_ref in ((gate0, up0), (gate1, up1)):
        gate = lax.dot_general(x, gate_ref[...], turned, preferred_element_type=F32)
        up = lax.dot_general(x, up_ref[...], turned, preferred_element_type=F32)
        hidden.append((gate / (1.0 + jnp.exp(-gate)) * up).astype(BF16))
    half = ROWS // 2
    low = lax.broadcasted_iota(jnp.int32, (half, LANES), 1) < 64
    for i in range(8):
        cols = slice(i * 256, (i + 1) * 256)
        part = jnp.dot(hidden[0], down0[:, cols], preferred_element_type=F32) + jnp.dot(hidden[1], down1[:, cols], preferred_element_type=F32)
        part = part * scale
        for b in range(2):
            one = part[:half, b * LANES : (b + 1) * LANES]
            two = part[half:, b * LANES : (b + 1) * LANES]
            mixed = pltpu.roll(jnp.where(low, two, one), 64, 1)
            out_ref[4 * i + 2 * b] = jnp.where(low, one, mixed).astype(BF16)
            out_ref[4 * i + 2 * b + 1] = jnp.where(low, mixed, two).astype(BF16)


def sum_kernel(in_ref, out_ref):
    sums = []
    for core in range(2):
        total = 0.0
        for q in range(CHIPS):
            total = total + in_ref[(q // 4 * 2 + core) * 4 + q % 4].astype(F32)
        sums.append(total)
    one, two = sums
    low = lax.broadcasted_iota(jnp.int32, one.shape, 1) < 64
    mixed = pltpu.roll(jnp.where(low, two, one), 64, 1)
    rows = (jnp.where(low, one, mixed).astype(BF16), jnp.where(low, mixed, two).astype(BF16))
    turn, stay = TURN * HALF, rows[0].shape[0] - TURN * HALF
    for half in range(2):
        out_ref[half, turn:] = rows[half][:stay]
        out_ref[1 - half, :turn] = rows[half][stay:]


def mix_kernel(in_ref, pos_ref, out_ref):
    tokens = pos_ref.shape[1]
    pos = pos_ref[...]
    seat = lax.broadcasted_iota(jnp.int32, (1, HALF, 1), 1)
    values = in_ref[...]
    parts = []
    for core in range(2):
        seated = pos[:, None, :] == (seat + core * HALF).astype(F32)
        seated = jnp.where(seated, 1.0, 0.0).reshape(ROWS, tokens).astype(BF16)
        parts.append(
            lax.dot_general(
                values, seated, (((0,), (0,)), ((), ())), preferred_element_type=F32
            )
        )
    out_ref[...] = (parts[0][0:64] + parts[1][64:128]).astype(BF16)


def call(kernel, outs, *args, specs=None, cost=None):
    shapes = [jax.ShapeDtypeStruct(s, d) for s, d in outs]
    many = len(shapes) > 1
    return pl.pallas_call(
        kernel,
        out_shape=shapes if many else shapes[0],
        in_specs=specs or [VMEM] * len(args),
        out_specs=[VMEM] * len(shapes) if many else VMEM,
        compiler_params=PARAMS,
        cost_estimate=cost,
    )(*args)


def per_device(tokens, expert_ids, route_weight, gate_weight, up_weight, down_weight):
    x, core, column = lax.axis_index("x"), lax.axis_index("core"), lax.axis_index("cuts")
    exchange = functools.partial(lax.all_to_all, split_axis=0, concat_axis=0, tiled=True)
    out_ring = [[(FIRST + i) % NODES for i in range(NODES)]]
    back_ring = [[(BACK + i) % NODES for i in range(NODES)]]
    weights = (gate_weight[0].T, up_weight[0].T, down_weight[0])
    pairs = [(0, 1), (1, 0)]
    weights = weights + tuple(lax.ppermute(w, "core", pairs) for w in weights)
    chip = column * 4 + x
    block = lax.dynamic_slice_in_dim(tokens, chip * LANES, LANES, axis=1)
    where = jnp.stack([core, column]).astype(jnp.int32)
    seats, scale, pos = call(
        seat_kernel,
        [
            ((ROWS, tokens.shape[0]), BF16),
            ((2, NODES, LANES), BF16),
            ((NODES, tokens.shape[0]), F32),
        ],
        where,
        expert_ids.T,
        route_weight.T,
        specs=[SMEM, VMEM, VMEM],
    )
    seats = call(pick_kernel, [((NODES, HALF, LANES), BF16)], seats, block)
    scale = jnp.swapaxes(scale, 0, 1).reshape(NODES, 1, 2, LANES)
    seats = jnp.concatenate([seats.reshape(NODES, 4, 2, LANES), scale], axis=1)
    seats = exchange(seats, "node", axis_index_groups=out_ring)
    scale = seats[:, 4, 0].astype(F32) + seats[:, 4, 1].astype(F32)
    copies = call(
        copies_kernel,
        [((CHIPS, ROWS, LANES), BF16)],
        seats[:, :4].reshape(NODES, HALF, LANES),
        cost=pl.CostEstimate(flops=1 << 20, bytes_accessed=1 << 20, transcendentals=0),
    )
    copies, scale, weights = lax.optimization_barrier((copies, scale, weights))
    rows = exchange(copies, ("cuts", "x"))
    plane = ("x", "core", "cuts")
    parts = call(expert_kernel, [((2 * CHIPS, ROWS // 2, LANES), BF16)], rows, scale, *weights)
    parts = exchange(parts, plane)
    total = call(sum_kernel, [((2, ROWS // 2, LANES), BF16)], parts)
    answers = exchange(
        total.reshape(NODES, HALF, LANES), "node", axis_index_groups=back_ring
    )
    mixed = call(mix_kernel, [((64, tokens.shape[0]), BF16)], answers.reshape(ROWS, LANES), pos)
    return mixed.T


def solution(mesh):
    fine = Mesh(mesh.devices.reshape(NODES, 4, 2, 4), ("node", "x", "core", "cuts"))
    in_specs = (
        P("node", None),
        P("node", None),
        P("node", None),
        P(("node", "cuts"), None, ("x", "core")),
        P(("node", "cuts"), None, ("x", "core")),
        P(("node", "cuts"), ("x", "core"), None),
    )
    out_specs = P("node", ("x", "core", "cuts"))
    return jax.shard_map(
        per_device, mesh=fine, in_specs=in_specs, out_specs=out_specs, check_vma=False
    )
```
